32 devices in a mesh: item: 8 (over y, x, core), tbl: 4 (over z).
Axes of the slice: x: 2, y: 2, z: 4, core: 2. Of those that a mesh axis runs over, the one named last changes fastest.
Arguments:
- tables: bfloat16 [8, 8192, 128], P('tbl'), may hold values from -2.5 to 2.5
- feat_ids: int32 [32768, 8, 8], P('item', 'tbl'), may hold values from 0 to 8191
- bag_lens: int32 [32768, 8], P('item', 'tbl'), may hold values from 1 to 8
- w_hidden: bfloat16 [1024, 1024], replicated, may hold values from -0.1875 to 0.1875
- b_hidden: float32 [1024], replicated, may hold values from -3 to 3
- w_out: bfloat16 [1024, 256], replicated, may hold values from -0.1875 to 0.1875
- b_out: float32 [256], replicated, may hold values from -3 to 3
- item_vecs: bfloat16 [2048, 256], P('item'), may hold values from -30 to 30
- elig_mask: int32 [64, 16], P(('item', 'tbl')), may hold values from 0 to 1, as said below
- positives: int32 [32768], P(('item', 'tbl')), may hold values from 0 to 2047, as said below
Outputs:
- user_loss: float32 [32768], P(('item', 'tbl'))
- user_grad: float32 [32768, 256], P(('item', 'tbl'))
- item_grad: float32 [2048, 256], P(('item', 'tbl'))
The draws below stay inside these ranges and needn't reach their ends.
Inputs may be any that keep to these rules, and one draw needn't show every extreme that they name: Every row of elig_mask holds at least one 1. elig_mask[u // 512, positives[u] // 128] = 1 for every user u.
All inputs are finite; a program needn't handle non-finite values.
Results may differ from the reference program's by a relative error of at most 0.03.
Values may be sent and summed in bfloat16 or wider, within the bound.
A program may use at most 64 MiB of HBM per device.

```python
import math
import jax
import jax.numpy as jnp
import numpy as np
from jax import lax

E = 128
ROWS = 8192
BAG = 8
HID = 1024
DQ = 256
UBLK = 512
IBLK = 128
FEATS = 8
USERS = 32768
ITEMS = 2048


def eligibility(key):
    block_count = USERS // UBLK
    column_count = ITEMS // IBLK
    key_list = jax.random.split(jax.random.fold_in(key, 11), 5)
    density = jax.random.randint(key_list[0], (block_count, 1), 10, 101)
    rolled = jax.random.randint(key_list[1], (block_count, column_count), 0, 100)
    forced = jax.random.randint(key_list[2], (block_count, 1), 0, column_count)
    columns = jnp.arange(column_count, dtype=jnp.int32)[None, :]
    eligible = jnp.logical_or(rolled < density, columns == forced).astype(jnp.int32)
    counts = jnp.sum(eligible, axis=1)
    rank_table = jnp.cumsum(eligible, axis=1) - 1
    owner_block = jnp.arange(USERS, dtype=jnp.int32) // UBLK
    pick_rank = jax.random.randint(key_list[3], (USERS,), 0, 1048576) % counts[owner_block]
    user_rows = eligible[owner_block]
    user_ranks = rank_table[owner_block]
    chosen = jnp.sum(jnp.where(jnp.logical_and(user_rows > 0, user_ranks == pick_rank[:, None]), columns, 0), axis=1)
    within = jax.random.randint(key_list[4], (USERS,), 0, IBLK)
    return (eligible, (chosen * IBLK + within).astype(jnp.int32))


def draw_elig_mask(key, part):
    return eligibility(key)[0]


def draw_positives(key, part):
    return eligibility(key)[1]


def draw_item_vecs(key, part):
    key_list = jax.random.split(jax.random.fold_in(key, 23), 1)
    return (jax.random.normal(key_list[0], (ITEMS, DQ), jnp.float32) * 0.1).astype(jnp.bfloat16)


def place_ends(entries, own_key, low, high):
    longest = entries.shape.index(max(entries.shape))
    spots = []
    for shift in (0, 1):
        where = [jax.random.randint(jax.random.fold_in(own_key, axis), (), 0, length) for axis, length in enumerate(entries.shape)]
        where[longest] = (where[longest] + shift) % entries.shape[longest]
        spots.append(tuple(where))
    return entries.at[spots[0]].set(low).at[spots[1]].set(high)


def level_of(own_key, shape, cuts, least, top_value):
    level = 1.0
    for position, blocks in cuts:
        steps = jax.random.uniform(jax.random.fold_in(jax.random.fold_in(own_key, 6), position), (blocks,), jnp.float32, least / len(cuts), top_value / len(cuts))
        level = level * jnp.repeat(jnp.exp(steps), shape[position] // blocks).reshape((-1,) + (1,) * (len(shape) - 1 - position))
    return level


def cumulative_ranks(number_of, lean):
    portions = [(1 << 20) // math.isqrt(rank ** lean) + 1 for rank in range(1, number_of + 1)]
    scale = 1 + sum(portions) // (1 << 30)
    return np.cumsum(np.array([max(1, weight // scale) for weight in portions]))


def ranked(key, extent, amount, skew):
    table = cumulative_ranks(amount, skew)
    pick = jax.random.randint(jax.random.fold_in(key, 1), extent, 0, int(table[amount - 1]))
    grade = jnp.searchsorted(jnp.asarray(table, jnp.int32), pick, side="right")
    return jax.random.permutation(jax.random.fold_in(key, 2), amount)[grade].astype(jnp.int32)


def gaussian(rng, shape, spread, most, cuts=(), kind=jnp.bfloat16):
    drawn = jax.random.normal(rng, shape, jnp.float32) * spread
    if len(cuts) > 0:
        drawn = level_of(rng, shape, cuts, -0.22, 0.18) * drawn
    return jnp.clip(drawn, min=-most, max=most).astype(kind)


def setup_inputs(seed: int = 0) -> dict:
    key_of = jax.random.split(jax.random.key(seed), 11)
    return {
        "tables": gaussian(key_of[0], (FEATS, ROWS, E), 0.35, 2.5, ((0, 4),)),
        "feat_ids": place_ends(ranked(key_of[1], (USERS, FEATS, BAG), ROWS, 2), jax.random.fold_in(key_of[1], 3), 0, ROWS - 1).astype(jnp.int32),
        "bag_lens": place_ends(jax.random.randint(key_of[2], (USERS, FEATS), 1, BAG + 1), jax.random.fold_in(key_of[2], 1), 1, BAG).astype(jnp.int32),
        "w_hidden": gaussian(key_of[3], (FEATS * E, HID), (FEATS * E) ** -0.5, 0.1875),
        "b_hidden": gaussian(key_of[4], (HID,), 0.5, 3.0, (), jnp.float32),
        "w_out": gaussian(key_of[5], (HID, DQ), HID ** -0.5, 0.1875),
        "b_out": gaussian(key_of[6], (DQ,), 0.3, 3.0, (), jnp.float32),
        "item_vecs": draw_item_vecs(jax.random.fold_in(key_of[10], 71), 0),
        "elig_mask": draw_elig_mask(jax.random.fold_in(key_of[10], 71), 0),
        "positives": draw_positives(jax.random.fold_in(key_of[10], 71), 0),
    }


masked_value = -1.0e30


def pool_feature(table, bag_ids, bag_count):
    gathered = jnp.take(table, bag_ids, axis=0).astype(jnp.float32)
    in_bag = jnp.arange(BAG, dtype=jnp.int32)[None, :] < bag_count[:, None]
    return jnp.sum(jnp.where(in_bag[:, :, None], gathered, 0.0), axis=1).astype(jnp.bfloat16)


def reference(tables, feat_ids, bag_lens, w_hidden, b_hidden, w_out, b_out, item_vecs, elig_mask, positives):
    pooled = lax.map(lambda feature: pool_feature(tables[feature], feat_ids[:, feature, :], bag_lens[:, feature]), jnp.arange(FEATS, dtype=jnp.int32))
    features = jnp.transpose(pooled, (1, 0, 2)).reshape(USERS, FEATS * E)
    hidden = jnp.maximum(jnp.dot(features, w_hidden, preferred_element_type=jnp.float32) + b_hidden, 0.0).astype(jnp.bfloat16)
    queries = (jnp.dot(hidden, w_out, preferred_element_type=jnp.float32) + b_out).astype(jnp.bfloat16)
    item_index = jnp.arange(ITEMS, dtype=jnp.int32)

    def user_block(item_grads, block_number):
        block_queries = lax.dynamic_slice_in_dim(queries, block_number * UBLK, UBLK, 0)
        wanted = lax.dynamic_slice_in_dim(positives, block_number * UBLK, UBLK, 0)
        allowed = jnp.repeat(elig_mask[block_number] > 0, IBLK)
        scores = jnp.dot(block_queries, item_vecs.T, preferred_element_type=jnp.float32)
        block_max = jnp.max(jnp.where(allowed[None, :], scores, masked_value), axis=1)
        totals = jnp.sum(jnp.where(allowed[None, :], jnp.exp(scores - block_max[:, None]), 0.0), axis=1)
        log_norm = block_max + jnp.log(totals)
        target = item_index[None, :] == wanted[:, None]
        picked = jnp.sum(jnp.where(target, scores, 0.0), axis=1)
        probabilities = jnp.where(allowed[None, :], jnp.exp(scores - log_norm[:, None]), 0.0)
        signal = (probabilities - target.astype(jnp.float32)).astype(jnp.bfloat16)
        user_part = jnp.dot(signal, item_vecs, preferred_element_type=jnp.float32)
        item_grads = item_grads + jnp.dot(signal.T, block_queries, preferred_element_type=jnp.float32)
        return item_grads, (log_norm - picked, user_part)

    item_grad, (losses, user_parts) = lax.scan(user_block, jnp.zeros((ITEMS, DQ), jnp.float32), jnp.arange(USERS // UBLK, dtype=jnp.int32))
    return losses.reshape(USERS), user_parts.reshape(USERS, DQ), item_grad
```

```python
import functools

import jax
import jax.numpy as jnp
from jax import lax
from jax.experimental import pallas as pl
from jax.experimental.pallas import tpu as pltpu
from jax.sharding import PartitionSpec as P

masked_value = -1e30
MIB = 1 << 20
MESH = pl.DeviceIdType.MESH


def pool_kernel(features, bag, ids_ref, table_ref, out_ref, sums_ref):
    users = out_ref.shape[0]
    width = table_ref.shape[2]

    def group(step, carry):
        first = pl.multiple_of(step * 8, 8)
        for user in range(8):
            for feature in range(features):
                rows = [
                    table_ref[ids_ref[(feature * bag + entry) * users + first + user]]
                    for entry in range(bag)
                ]
                while len(rows) > 1:
                    rows = [
                        rows[k] + rows[k + 1] if k + 1 < len(rows) else rows[k]
                        for k in range(0, len(rows), 2)
                    ]
                sums_ref[step, user : user + 1, feature * width : (feature + 1) * width] = rows[0]
        return carry

    lax.fori_loop(0, users // 8, group, 0)
    out_ref[...] = sums_ref[...].reshape(out_ref.shape).astype(out_ref.dtype)


def pool_chunk(ids, table, users, features, bag):
    width = table.shape[2]
    return pl.pallas_call(
        functools.partial(pool_kernel, features, bag),
        out_shape=jax.ShapeDtypeStruct((users, features * width), jnp.bfloat16),
        in_specs=[
            pl.BlockSpec(memory_space=pltpu.SMEM),
            pl.BlockSpec(memory_space=pltpu.VMEM),
        ],
        out_specs=pl.BlockSpec(memory_space=pltpu.VMEM),
        scratch_shapes=[pltpu.VMEM((users // 8, 8, features * width), jnp.float32)],
        compiler_params=pltpu.CompilerParams(vmem_limit_bytes=20 * MIB),
        cost_estimate=pl.CostEstimate(
            flops=users * features * bag * width * 100, bytes_accessed=16 * MIB, transcendentals=0
        ),
        name="pool_chunk",
    )(ids, table)


def main_kernel(
    order, me_ref, elig_ref, *refs
):
    count = len(order)
    piece_refs = refs[:count]
    (w1_ref, b1_ref, w2_ref, b2_ref, items_ref, pos_ref, loss_ref, ugrad_ref, igrad_ref,
     scores_ref, signal_ref, acc_ref) = refs[count:]
    tile = pl.program_id(0)
    tile_users = ugrad_ref.shape[0]
    items = items_ref.shape[0]
    blocks = elig_ref.shape[1]
    iblk = items // blocks
    user_block = tile * elig_ref.shape[0] // pl.num_programs(0)
    depth = piece_refs[0].shape[1]
    me = me_ref[0]

    hidden = None
    for position, distance in enumerate(order):
        source = lax.rem(me - distance + count, count)
        weight = w1_ref[pl.ds(pl.multiple_of(source * depth, depth), depth), :]
        part = jnp.dot(piece_refs[position][...], weight, preferred_element_type=jnp.float32)
        hidden = part if hidden is None else hidden + part
    hidden = jnp.maximum(hidden + b1_ref[...], 0.0).astype(jnp.bfloat16)
    queries = (
        jnp.dot(hidden, w2_ref[...], preferred_element_type=jnp.float32) + b2_ref[...]
    ).astype(jnp.bfloat16)

    wanted = pos_ref[...]
    row = lax.broadcasted_iota(jnp.int32, (iblk, tile_users), 0)
    peak = jnp.full((8, tile_users), masked_value, jnp.float32)
    chosen = jnp.zeros((8, tile_users), jnp.float32)
    for block in range(blocks):
        span = slice(block * iblk, (block + 1) * iblk)
        scores = lax.dot_general(
            items_ref[span, :], queries, (((1,), (1,)), ((), ())),
            preferred_element_type=jnp.float32,
        )
        scores = jnp.where(elig_ref[user_block, block] > 0, scores, masked_value)
        target = row == wanted - block * iblk
        chosen += jnp.sum(
            jnp.where(target, scores, 0.0).reshape(iblk // 8, 8, tile_users), axis=0
        )
        peak = jnp.maximum(peak, jnp.max(scores.reshape(iblk // 8, 8, tile_users), axis=0))
        scores_ref[span, :] = scores
    peak = jnp.max(peak, axis=0, keepdims=True)
    chosen = jnp.sum(chosen, axis=0, keepdims=True)
    total = jnp.zeros((8, tile_users), jnp.float32)
    for block in range(blocks):
        span = slice(block * iblk, (block + 1) * iblk)
        weights = jnp.exp(scores_ref[span, :] - peak)
        total += jnp.sum(weights.reshape(iblk // 8, 8, tile_users), axis=0)
        scores_ref[span, :] = weights
    total = jnp.sum(total, axis=0, keepdims=True)
    loss_ref[...] = peak + jnp.log(total) - chosen
    inverse = 1.0 / total
    for block in range(blocks):
        span = slice(block * iblk, (block + 1) * iblk)
        target = row == wanted - block * iblk
        signal_ref[span, :] = (
            scores_ref[span, :] * inverse - target.astype(jnp.float32)
        ).astype(jnp.bfloat16)
    ugrad_ref[...] = lax.dot_general(
        signal_ref[...], items_ref[...], (((0,), (0,)), ((), ())),
        preferred_element_type=jnp.float32,
    )
    part = jnp.dot(signal_ref[...], queries, preferred_element_type=jnp.float32)

    @pl.when(tile == 0)
    def _():
        acc_ref[...] = part

    @pl.when(tile > 0)
    def _():
        acc_ref[...] += part

    @pl.when(tile == pl.num_programs(0) - 1)
    def _():
        igrad_ref[...] = acc_ref[...].astype(igrad_ref.dtype)


def main_call(order, me, pieces, w_hidden, b_hidden, w_out, b_out, items, elig, positives):
    users, depth = pieces[0].shape
    tile_users = 256
    tiles = users // tile_users
    count, width = items.shape
    hid = w_hidden.shape[1]
    whole = lambda shape: pl.BlockSpec(shape, lambda i: (0, 0))
    smem = pl.BlockSpec(memory_space=pltpu.SMEM)
    return pl.pallas_call(
        functools.partial(main_kernel, order),
        grid=(tiles,),
        out_shape=(
            jax.ShapeDtypeStruct((1, users), jnp.float32),
            jax.ShapeDtypeStruct((users, width), jnp.float32),
            jax.ShapeDtypeStruct((count, width), jnp.bfloat16),
        ),
        in_specs=[smem, smem]
        + [pl.BlockSpec((tile_users, depth), lambda i: (i, 0))] * len(order)
        + [
            whole(w_hidden.shape),
            whole((1, hid)),
            whole(w_out.shape),
            whole((1, width)),
            whole((count, width)),
            pl.BlockSpec((1, tile_users), lambda i: (0, i)),
        ],
        out_specs=(
            pl.BlockSpec((1, tile_users), lambda i: (0, i)),
            pl.BlockSpec((tile_users, width), lambda i: (i, 0)),
            whole((count, width)),
        ),
        scratch_shapes=[
            pltpu.VMEM((count, tile_users), jnp.float32),
            pltpu.VMEM((count, tile_users), jnp.bfloat16),
            pltpu.VMEM((count, width), jnp.float32),
        ],
        compiler_params=pltpu.CompilerParams(vmem_limit_bytes=48 * MIB),
        name="tower_and_softmax",
    )(
        me, elig, *pieces, w_hidden, b_hidden.reshape(1, hid), w_out, b_out.reshape(1, width),
        items, positives.reshape(1, users),
    )


def reduce_kernel(
    chips, shards, part_ref, out_ref, got_a, sum_a, got_b, sum_b, got_c,
    send_a, recv_a, send_b, recv_b, send_c, recv_c,
):
    item = lax.axis_index("item")
    shard = lax.axis_index("tbl")
    core = lax.rem(item, 2)
    chip = item // 2
    other_core = (2 * chip + 1 - core, shard)
    chip_at = lambda k: (2 * lax.rem(chip + k, chips) + core, shard)
    shard_at = lambda k: (item, lax.rem(shard + k, shards))
    partners = (
        [other_core]
        + [chip_at(k) for k in range(1, chips)]
        + [shard_at(k) for k in range(1, shards)]
    )
    barrier = pltpu.get_barrier_semaphore()
    for partner in partners:
        pl.semaphore_signal(barrier, inc=1, device_id=partner, device_id_type=MESH)
    pl.semaphore_wait(barrier, len(partners))

    copy = pltpu.make_async_remote_copy(
        src_ref=part_ref.at[:, 1 - core], dst_ref=got_a, send_sem=send_a, recv_sem=recv_a,
        device_id=other_core, device_id_type=MESH,
    )
    copy.start()
    copy.wait()
    sum_a[...] = (
        part_ref[:, core].astype(jnp.float32) + got_a[...].astype(jnp.float32)
    ).astype(sum_a.dtype)

    copies = []
    for k in range(1, chips):
        copies.append(pltpu.make_async_remote_copy(
            src_ref=sum_a.at[lax.rem(chip + k, chips)], dst_ref=got_b.at[k - 1],
            send_sem=send_b.at[k - 1], recv_sem=recv_b.at[k - 1],
            device_id=chip_at(k), device_id_type=MESH,
        ))
        copies[-1].start()
    total = sum_a[chip].astype(jnp.float32)
    for k in range(1, chips):
        copies[k - 1].wait()
        total += got_b[k - 1].astype(jnp.float32)
    rows = out_ref.shape[0]
    sum_b[...] = total.astype(sum_b.dtype).reshape(shards, rows, total.shape[1])

    copies = []
    for k in range(1, shards):
        copies.append(pltpu.make_async_remote_copy(
            src_ref=sum_b.at[lax.rem(shard + k, shards)], dst_ref=got_c.at[k - 1],
            send_sem=send_c.at[k - 1], recv_sem=recv_c.at[k - 1],
            device_id=shard_at(k), device_id_type=MESH,
        ))
        copies[-1].start()
    total = sum_b[shard].astype(jnp.float32)
    for k in range(1, shards):
        copies[k - 1].wait()
        total += got_c[k - 1].astype(jnp.float32)
    out_ref[...] = total


def reduce_call(partial):
    chips, _, rows, width = partial.shape
    shards = lax.axis_size("tbl")
    piece = rows // shards
    dma = pltpu.SemaphoreType.DMA
    return pl.pallas_call(
        functools.partial(reduce_kernel, chips, shards),
        out_shape=jax.ShapeDtypeStruct((piece, width), jnp.float32),
        in_specs=[pl.BlockSpec(memory_space=pltpu.VMEM)],
        out_specs=pl.BlockSpec(memory_space=pltpu.VMEM),
        scratch_shapes=[
            pltpu.VMEM((chips, rows, width), jnp.bfloat16),
            pltpu.VMEM((chips, rows, width), jnp.bfloat16),
            pltpu.VMEM((chips - 1, rows, width), jnp.bfloat16),
            pltpu.VMEM((shards, piece, width), jnp.bfloat16),
            pltpu.VMEM((shards - 1, piece, width), jnp.bfloat16),
            dma, dma,
            dma((chips - 1,)), dma((chips - 1,)),
            dma((shards - 1,)), dma((shards - 1,)),
        ],
        compiler_params=pltpu.CompilerParams(
            collective_id=0, has_side_effects=True, vmem_limit_bytes=24 * MIB
        ),
        name="reduce_item_grad",
    )(partial)


def local(
    tables, feat_ids, bag_lens, w_hidden, b_hidden, w_out, b_out, item_vecs, elig_mask, positives
):
    shards = lax.axis_size("tbl")
    me = lax.axis_index("tbl")
    group_users, features, bag = feat_ids.shape
    users = group_users // shards
    rows, width = tables.shape[1:]

    items = lax.all_gather(item_vecs, "item", axis=0, tiled=True)

    zero_row = features * rows
    table = jnp.concatenate(
        [
            tables.astype(jnp.float32).reshape(zero_row, 1, width),
            jnp.zeros((8, 1, width), jnp.float32),
        ]
    )
    ids = jnp.transpose(feat_ids, (1, 2, 0))
    lens = jnp.transpose(bag_lens, (1, 0))
    in_bag = jnp.arange(bag, dtype=jnp.int32)[None, :, None] < lens[:, None, :]
    base = (jnp.arange(features, dtype=jnp.int32) * rows)[:, None, None]
    ids = jnp.where(in_bag, ids + base, zero_row)
    ids = jnp.transpose(ids.reshape(features * bag, shards, users), (1, 0, 2))
    ids = ids.reshape(shards, features * bag * users)

    order = sorted(range(1, shards), key=lambda d: (abs(2 * d - shards), d)) + [0]
    pieces = []
    for distance in order:
        target = lax.rem(me + distance, shards)
        chunk = lax.dynamic_index_in_dim(ids, target, 0, keepdims=False)
        pooled = pool_chunk(chunk, table, users, features, bag)
        if distance:
            pairs = [(source, (source + distance) % shards) for source in range(shards)]
            pooled = lax.ppermute(pooled, "tbl", pairs)
        pieces.append(pooled)

    loss, user_grad, partial = main_call(
        tuple(order), me.reshape(1).astype(jnp.int32), pieces, w_hidden, b_hidden, w_out, b_out,
        items, elig_mask, positives,
    )
    cycle = lax.axis_size("item")
    partial = partial.reshape(cycle // 2, 2, item_vecs.shape[0], item_vecs.shape[1])
    item_grad = reduce_call(partial)
    return (loss.reshape(users), user_grad, item_grad)


def solution(mesh):
    in_specs = (
        P("tbl", None, None),
        P("item", "tbl", None),
        P("item", "tbl"),
        P(),
        P(),
        P(),
        P(),
        P("item", None),
        P(("item", "tbl"), None),
        P(("item", "tbl")),
    )
    out_specs = (P(("item", "tbl")), P(("item", "tbl"), None), P(("item", "tbl"), None))
    return jax.shard_map(local, mesh=mesh, in_specs=in_specs, out_specs=out_specs, check_vma=False)
```

```python
import functools

import jax
import jax.numpy as jnp
from jax import lax
from jax.experimental import pallas as pl
from jax.experimental.pallas import tpu as pltpu
from jax.sharding import PartitionSpec as P

masked_value = -1e30
MIB = 1 << 20
MESH = pl.DeviceIdType.MESH


def pool_kernel(features, bag, ids_ref, table_ref, out_ref, sums_ref):
    users = out_ref.shape[0]
    width = table_ref.shape[2]

    def group(step, carry):
        first = pl.multiple_of(step * 8, 8)
        for user in range(8):
            for feature in range(features):
                rows = [
                    table_ref[ids_ref[first + ((feature * bag + entry) * users + user)]]
                    for entry in range(bag)
                ]
                while len(rows) > 1:
                    rows = [
                        rows[k] + rows[k + 1] if k + 1 < len(rows) else rows[k]
                        for k in range(0, len(rows), 2)
                    ]
                sums_ref[step, user : user + 1, feature * width : (feature + 1) * width] = rows[0]
        return carry

    lax.fori_loop(0, users // 8, group, 0)
    out_ref[...] = sums_ref[...].reshape(out_ref.shape).astype(out_ref.dtype)


def pool_chunk(ids, table, users, features, bag):
    width = table.shape[2]
    return pl.pallas_call(
        functools.partial(pool_kernel, features, bag),
        out_shape=jax.ShapeDtypeStruct((users, features * width), jnp.bfloat16),
        in_specs=[
            pl.BlockSpec(memory_space=pltpu.SMEM),
            pl.BlockSpec(memory_space=pltpu.VMEM),
        ],
        out_specs=pl.BlockSpec(memory_space=pltpu.VMEM),
        scratch_shapes=[pltpu.VMEM((users // 8, 8, features * width), jnp.float32)],
        compiler_params=pltpu.CompilerParams(vmem_limit_bytes=20 * MIB),
        cost_estimate=pl.CostEstimate(
            flops=users * features * bag * width * 100, bytes_accessed=16 * MIB, transcendentals=0
        ),
        name="pool_chunk",
    )(ids, table)


def main_kernel(order, owned, me_ref, elig_ref, *refs):
    count = len(order)
    piece_refs = refs[:count]
    (w1_ref, b1_ref, w2_ref, b2_ref, mixed_ref, pos_ref, loss_ref, ugrad_ref, igrad_ref,
     items_ref, scores_ref, signal_ref, acc_ref) = refs[count:]
    tile = pl.program_id(0)
    tile_users = ugrad_ref.shape[0]
    items = items_ref.shape[0]
    blocks = elig_ref.shape[1]
    iblk = items // blocks
    user_block = tile * elig_ref.shape[0] // pl.num_programs(0)
    depth = piece_refs[0].shape[1]
    me = me_ref[0]

    @pl.when(tile == 0)
    def _():
        for owner in range(items // owned):
            place = pl.multiple_of((me_ref[1] ^ owner) * owned, owned)
            items_ref[owner * owned : (owner + 1) * owned, :] = mixed_ref[pl.ds(place, owned), :]

    hidden = None
    for position, distance in enumerate(order):
        source = lax.rem(me - distance + count, count)
        weight = w1_ref[pl.ds(pl.multiple_of(source * depth, depth), depth), :]
        part = jnp.dot(piece_refs[position][...], weight, preferred_element_type=jnp.float32)
        hidden = part if hidden is None else hidden + part
    hidden = jnp.maximum(hidden + b1_ref[...], 0.0).astype(jnp.bfloat16)
    queries = (
        jnp.dot(hidden, w2_ref[...], preferred_element_type=jnp.float32) + b2_ref[...]
    ).astype(jnp.bfloat16)

    wanted = pos_ref[...]
    row = lax.broadcasted_iota(jnp.int32, (iblk, tile_users), 0)
    peak = jnp.full((8, tile_users), masked_value, jnp.float32)
    chosen = jnp.zeros((8, tile_users), jnp.float32)
    for block in range(blocks):
        span = slice(block * iblk, (block + 1) * iblk)
        scores = lax.dot_general(
            items_ref[span, :], queries, (((1,), (1,)), ((), ())),
            preferred_element_type=jnp.float32,
        )
        scores = jnp.where(elig_ref[user_block, block] > 0, scores, masked_value)
        target = row == wanted - block * iblk
        chosen += jnp.sum(
            jnp.where(target, scores, 0.0).reshape(iblk // 8, 8, tile_users), axis=0
        )
        peak = jnp.maximum(peak, jnp.max(scores.reshape(iblk // 8, 8, tile_users), axis=0))
        scores_ref[span, :] = scores
    peak = jnp.max(peak, axis=0, keepdims=True)
    chosen = jnp.sum(chosen, axis=0, keepdims=True)
    total = jnp.zeros((8, tile_users), jnp.float32)
    for block in range(blocks):
        span = slice(block * iblk, (block + 1) * iblk)
        weights = jnp.exp(scores_ref[span, :] - peak)
        total += jnp.sum(weights.reshape(iblk // 8, 8, tile_users), axis=0)
        scores_ref[span, :] = weights
    total = jnp.sum(total, axis=0, keepdims=True)
    loss_ref[...] = peak + jnp.log(total) - chosen
    inverse = 1.0 / total
    for block in range(blocks):
        span = slice(block * iblk, (block + 1) * iblk)
        target = row == wanted - block * iblk
        signal_ref[span, :] = (
            scores_ref[span, :] * inverse - target.astype(jnp.float32)
        ).astype(jnp.bfloat16)
    ugrad_ref[...] = lax.dot_general(
        signal_ref[...], items_ref[...], (((0,), (0,)), ((), ())),
        preferred_element_type=jnp.float32,
    )
    part = jnp.dot(signal_ref[...], queries, preferred_element_type=jnp.float32)

    @pl.when(tile == 0)
    def _():
        acc_ref[...] = part

    @pl.when(tile > 0)
    def _():
        acc_ref[...] += part

    @pl.when(tile == pl.num_programs(0) - 1)
    def _():
        igrad_ref[...] = acc_ref[...].astype(igrad_ref.dtype)


def main_call(order, owned, me, pieces, w_hidden, b_hidden, w_out, b_out, items, elig, positives):
    users, depth = pieces[0].shape
    tile_users = 256
    tiles = users // tile_users
    count, width = items.shape
    hid = w_hidden.shape[1]
    whole = lambda shape: pl.BlockSpec(shape, lambda i: (0, 0))
    smem = pl.BlockSpec(memory_space=pltpu.SMEM)
    return pl.pallas_call(
        functools.partial(main_kernel, order, owned),
        grid=(tiles,),
        out_shape=(
            jax.ShapeDtypeStruct((1, users), jnp.float32),
            jax.ShapeDtypeStruct((users, width), jnp.float32),
            jax.ShapeDtypeStruct((count, width), jnp.bfloat16),
        ),
        in_specs=[smem, smem]
        + [pl.BlockSpec((tile_users, depth), lambda i: (i, 0))] * len(order)
        + [
            whole(w_hidden.shape),
            whole((1, hid)),
            whole(w_out.shape),
            whole((1, width)),
            whole((count, width)),
            pl.BlockSpec((1, tile_users), lambda i: (0, i)),
        ],
        out_specs=(
            pl.BlockSpec((1, tile_users), lambda i: (0, i)),
            pl.BlockSpec((tile_users, width), lambda i: (i, 0)),
            whole((count, width)),
        ),
        scratch_shapes=[
            pltpu.VMEM((count, width), jnp.bfloat16),
            pltpu.VMEM((count, tile_users), jnp.float32),
            pltpu.VMEM((count, tile_users), jnp.bfloat16),
            pltpu.VMEM((count, width), jnp.float32),
        ],
        compiler_params=pltpu.CompilerParams(vmem_limit_bytes=48 * MIB),
        name="tower_and_softmax",
    )(
        me, elig, *pieces, w_hidden, b_hidden.reshape(1, hid), w_out, b_out.reshape(1, width),
        items, positives.reshape(1, users),
    )


def reduce_kernel(
    chips, shards, part_ref, out_ref, got_a, sum_a, got_b, sum_b, got_c,
    send_a, recv_a, send_b, recv_b, send_c, recv_c,
):
    item = lax.axis_index("item")
    shard = lax.axis_index("tbl")
    core = lax.rem(item, 2)
    chip = item // 2
    other_core = (2 * chip + 1 - core, shard)
    chip_at = lambda k: (2 * lax.rem(chip + k, chips) + core, shard)
    shard_at = lambda k: (item, lax.rem(shard + k, shards))
    partners = (
        [other_core]
        + [chip_at(k) for k in range(1, chips)]
        + [shard_at(k) for k in range(1, shards)]
    )
    barrier = pltpu.get_barrier_semaphore()
    for partner in partners:
        pl.semaphore_signal(barrier, inc=1, device_id=partner, device_id_type=MESH)
    pl.semaphore_wait(barrier, len(partners))

    copy = pltpu.make_async_remote_copy(
        src_ref=part_ref.at[:, 1 - core], dst_ref=got_a, send_sem=send_a, recv_sem=recv_a,
        device_id=other_core, device_id_type=MESH,
    )
    copy.start()
    copy.wait()
    sum_a[...] = (
        part_ref[:, core].astype(jnp.float32) + got_a[...].astype(jnp.float32)
    ).astype(sum_a.dtype)

    copies = []
    for k in range(1, chips):
        copies.append(pltpu.make_async_remote_copy(
            src_ref=sum_a.at[lax.rem(chip + k, chips)], dst_ref=got_b.at[k - 1],
            send_sem=send_b.at[k - 1], recv_sem=recv_b.at[k - 1],
            device_id=chip_at(k), device_id_type=MESH,
        ))
        copies[-1].start()
    total = sum_a[chip].astype(jnp.float32)
    for k in range(1, chips):
        copies[k - 1].wait()
        total += got_b[k - 1].astype(jnp.float32)
    rows = out_ref.shape[0]
    sum_b[...] = total.astype(sum_b.dtype).reshape(shards, rows, total.shape[1])

    copies = []
    for k in range(1, shards):
        copies.append(pltpu.make_async_remote_copy(
            src_ref=sum_b.at[lax.rem(shard + k, shards)], dst_ref=got_c.at[k - 1],
            send_sem=send_c.at[k - 1], recv_sem=recv_c.at[k - 1],
            device_id=shard_at(k), device_id_type=MESH,
        ))
        copies[-1].start()
    total = sum_b[shard].astype(jnp.float32)
    for k in range(1, shards):
        copies[k - 1].wait()
        total += got_c[k - 1].astype(jnp.float32)
    out_ref[...] = total


def reduce_call(partial):
    chips, _, rows, width = partial.shape
    shards = lax.axis_size("tbl")
    piece = rows // shards
    dma = pltpu.SemaphoreType.DMA
    return pl.pallas_call(
        functools.partial(reduce_kernel, chips, shards),
        out_shape=jax.ShapeDtypeStruct((piece, width), jnp.float32),
        in_specs=[pl.BlockSpec(memory_space=pltpu.VMEM)],
        out_specs=pl.BlockSpec(memory_space=pltpu.VMEM),
        scratch_shapes=[
            pltpu.VMEM((chips, rows, width), jnp.bfloat16),
            pltpu.VMEM((chips, rows, width), jnp.bfloat16),
            pltpu.VMEM((chips - 1, rows, width), jnp.bfloat16),
            pltpu.VMEM((shards, piece, width), jnp.bfloat16),
            pltpu.VMEM((shards - 1, piece, width), jnp.bfloat16),
            dma, dma,
            dma((chips - 1,)), dma((chips - 1,)),
            dma((shards - 1,)), dma((shards - 1,)),
        ],
        compiler_params=pltpu.CompilerParams(
            collective_id=0, has_side_effects=True, vmem_limit_bytes=24 * MIB
        ),
        name="reduce_item_grad",
    )(partial)


def local(
    tables, feat_ids, bag_lens, w_hidden, b_hidden, w_out, b_out, item_vecs, elig_mask, positives
):
    shards = lax.axis_size("tbl")
    me = lax.axis_index("tbl")
    group_users, features, bag = feat_ids.shape
    users = group_users // shards
    rows, width = tables.shape[1:]

    cycle = lax.axis_size("item")
    items = item_vecs
    reach = 1
    while reach < cycle:
        pairs = [(source, source ^ reach) for source in range(cycle)]
        items = jnp.concatenate([items, lax.ppermute(items, "item", pairs)])
        reach *= 2

    zero_row = features * rows
    table = jnp.pad(tables.reshape(zero_row, width).astype(jnp.float32), ((0, 8), (0, 0)))
    table = lax.optimization_barrier(table).reshape(zero_row + 8, 1, width)
    ids = jnp.transpose(feat_ids, (1, 2, 0))
    lens = jnp.transpose(bag_lens, (1, 0))
    in_bag = jnp.arange(bag, dtype=jnp.int32)[None, :, None] < lens[:, None, :]
    base = (jnp.arange(features, dtype=jnp.int32) * rows)[:, None, None]
    ids = jnp.where(in_bag, ids + base, zero_row)
    ids = jnp.transpose(ids.reshape(features * bag, shards, users), (1, 0, 2))
    ids = ids.reshape(shards, features * bag * users)

    order = sorted(range(1, shards), key=lambda d: (abs(2 * d - shards), d)) + [0]
    pieces = []
    for distance in order:
        target = lax.rem(me + distance, shards)
        chunk = lax.dynamic_index_in_dim(ids, target, 0, keepdims=False)
        pooled = pool_chunk(chunk, table, users, features, bag)
        if distance:
            pairs = [(source, (source + distance) % shards) for source in range(shards)]
            pooled = lax.ppermute(pooled, "tbl", pairs)
        pieces.append(pooled)

    loss, user_grad, partial = main_call(
        tuple(order), item_vecs.shape[0],
        jnp.stack([me, lax.axis_index("item")]).astype(jnp.int32), pieces, w_hidden, b_hidden, w_out, b_out,
        items, elig_mask, positives,
    )
    partial = partial.reshape(cycle // 2, 2, item_vecs.shape[0], item_vecs.shape[1])
    item_grad = reduce_call(partial)
    return (loss.reshape(users), user_grad, item_grad)


def solution(mesh):
    in_specs = (
        P("tbl", None, None),
        P("item", "tbl", None),
        P("item", "tbl"),
        P(),
        P(),
        P(),
        P(),
        P("item", None),
        P(("item", "tbl"), None),
        P(("item", "tbl")),
    )
    out_specs = (P(("item", "tbl")), P(("item", "tbl"), None), P(("item", "tbl"), None))
    return jax.shard_map(local, mesh=mesh, in_specs=in_specs, out_specs=out_specs, check_vma=False)
```

```python
import functools

import jax
import jax.numpy as jnp
from jax import lax
from jax.experimental import pallas as pl
from jax.experimental.pallas import tpu as pltpu
from jax.sharding import PartitionSpec as P

masked_value = -1e30
UNROLL = 32
MIB = 1 << 20
MESH = pl.DeviceIdType.MESH


def pool_kernel(features, bag, ids_ref, table_ref, out_ref, sums_ref):
    users = out_ref.shape[0]
    width = table_ref.shape[2]

    def group(step, carry):
        first = pl.multiple_of(step * UNROLL, UNROLL)
        for user in range(UNROLL):
            for feature in range(features):
                rows = [
                    table_ref[ids_ref[first + ((feature * bag + entry) * users + user)]]
                    for entry in range(bag)
                ]
                while len(rows) > 1:
                    rows = [
                        rows[k] + rows[k + 1] if k + 1 < len(rows) else rows[k]
                        for k in range(0, len(rows), 2)
                    ]
                sums_ref[step, user : user + 1, feature * width : (feature + 1) * width] = rows[0]
        return carry

    lax.fori_loop(0, users // UNROLL, group, 0)
    out_ref[...] = sums_ref[...].reshape(out_ref.shape).astype(out_ref.dtype)


def pool_chunk(ids, table, users, features, bag):
    width = table.shape[2]
    return pl.pallas_call(
        functools.partial(pool_kernel, features, bag),
        out_shape=jax.ShapeDtypeStruct((users, features * width), jnp.bfloat16),
        in_specs=[
            pl.BlockSpec(memory_space=pltpu.SMEM),
            pl.BlockSpec(memory_space=pltpu.VMEM),
        ],
        out_specs=pl.BlockSpec(memory_space=pltpu.VMEM),
        scratch_shapes=[pltpu.VMEM((users // UNROLL, UNROLL, features * width), jnp.float32)],
        compiler_params=pltpu.CompilerParams(vmem_limit_bytes=12 * MIB),
        cost_estimate=pl.CostEstimate(
            flops=users * features * bag * width * 100, bytes_accessed=16 * MIB, transcendentals=0
        ),
        name="pool_chunk",
    )(ids, table)


def main_kernel(order, owned, me_ref, elig_ref, *refs):
    count = len(order)
    piece_refs = refs[:count]
    (w1_ref, b1_ref, w2_ref, b2_ref, mixed_ref, pos_ref, loss_ref, ugrad_ref, igrad_ref,
     items_ref, scores_ref, signal_ref, acc_ref) = refs[count:]
    tile = pl.program_id(0)
    tile_users = ugrad_ref.shape[0]
    items = items_ref.shape[0]
    blocks = elig_ref.shape[1]
    iblk = items // blocks
    user_block = tile * elig_ref.shape[0] // pl.num_programs(0)
    depth = piece_refs[0].shape[1]
    me = me_ref[0]

    @pl.when(tile == 0)
    def _():
        for owner in range(items // owned):
            place = pl.multiple_of((me_ref[1] ^ owner) * owned, owned)
            items_ref[owner * owned : (owner + 1) * owned, :] = mixed_ref[pl.ds(place, owned), :]

    hidden = None
    for position, distance in enumerate(order):
        source = lax.rem(me - distance + count, count)
        weight = w1_ref[pl.ds(pl.multiple_of(source * depth, depth), depth), :]
        part = jnp.dot(piece_refs[position][...], weight, preferred_element_type=jnp.float32)
        hidden = part if hidden is None else hidden + part
    hidden = jnp.maximum(hidden + b1_ref[...], 0.0).astype(jnp.bfloat16)
    queries = (
        jnp.dot(hidden, w2_ref[...], preferred_element_type=jnp.float32) + b2_ref[...]
    ).astype(jnp.bfloat16)

    wanted = pos_ref[...]
    row = lax.broadcasted_iota(jnp.int32, (iblk, tile_users), 0)
    peak = jnp.full((8, tile_users), masked_value, jnp.float32)
    chosen = jnp.zeros((8, tile_users), jnp.float32)
    for block in range(blocks):
        span = slice(block * iblk, (block + 1) * iblk)
        scores = lax.dot_general(
            items_ref[span, :], queries, (((1,), (1,)), ((), ())),
            preferred_element_type=jnp.float32,
        )
        scores = jnp.where(elig_ref[user_block, block] > 0, scores, masked_value)
        target = row == wanted - block * iblk
        chosen += jnp.sum(
            jnp.where(target, scores, 0.0).reshape(iblk // 8, 8, tile_users), axis=0
        )
        peak = jnp.maximum(peak, jnp.max(scores.reshape(iblk // 8, 8, tile_users), axis=0))
        scores_ref[span, :] = scores
    peak = jnp.max(peak, axis=0, keepdims=True)
    chosen = jnp.sum(chosen, axis=0, keepdims=True)
    total = jnp.zeros((8, tile_users), jnp.float32)
    for block in range(blocks):
        span = slice(block * iblk, (block + 1) * iblk)
        weights = jnp.exp(scores_ref[span, :] - peak)
        total += jnp.sum(weights.reshape(iblk // 8, 8, tile_users), axis=0)
        scores_ref[span, :] = weights
    total = jnp.sum(total, axis=0, keepdims=True)
    loss_ref[...] = peak + jnp.log(total) - chosen
    inverse = 1.0 / total
    for block in range(blocks):
        span = slice(block * iblk, (block + 1) * iblk)
        target = row == wanted - block * iblk
        signal_ref[span, :] = (
            scores_ref[span, :] * inverse - target.astype(jnp.float32)
        ).astype(jnp.bfloat16)
    ugrad_ref[...] = lax.dot_general(
        signal_ref[...], items_ref[...], (((0,), (0,)), ((), ())),
        preferred_element_type=jnp.float32,
    )
    part = jnp.dot(signal_ref[...], queries, preferred_element_type=jnp.float32)

    @pl.when(tile == 0)
    def _():
        acc_ref[...] = part

    @pl.when(tile > 0)
    def _():
        acc_ref[...] += part

    @pl.when(tile == pl.num_programs(0) - 1)
    def _():
        half = igrad_ref.shape[2]
        for h in range(igrad_ref.shape[0]):
            igrad_ref[h] = acc_ref[:, h * half : (h + 1) * half].astype(igrad_ref.dtype)


def main_call(order, owned, me, pieces, w_hidden, b_hidden, w_out, b_out, items, elig, positives):
    users, depth = pieces[0].shape
    tile_users = 256
    tiles = users // tile_users
    count, width = items.shape
    hid = w_hidden.shape[1]
    whole = lambda shape: pl.BlockSpec(shape, lambda i: (0, 0))
    smem = pl.BlockSpec(memory_space=pltpu.SMEM)
    return pl.pallas_call(
        functools.partial(main_kernel, order, owned),
        grid=(tiles,),
        out_shape=(
            jax.ShapeDtypeStruct((1, users), jnp.float32),
            jax.ShapeDtypeStruct((users, width), jnp.float32),
            jax.ShapeDtypeStruct((2, count, width // 2), jnp.bfloat16),
        ),
        in_specs=[smem, smem]
        + [pl.BlockSpec((tile_users, depth), lambda i: (i, 0))] * len(order)
        + [
            whole(w_hidden.shape),
            whole((1, hid)),
            whole(w_out.shape),
            whole((1, width)),
            whole((count, width)),
            pl.BlockSpec((1, tile_users), lambda i: (0, i)),
        ],
        out_specs=(
            pl.BlockSpec((1, tile_users), lambda i: (0, i)),
            pl.BlockSpec((tile_users, width), lambda i: (i, 0)),
            pl.BlockSpec((2, count, width // 2), lambda i: (0, 0, 0)),
        ),
        scratch_shapes=[
            pltpu.VMEM((count, width), jnp.bfloat16),
            pltpu.VMEM((count, tile_users), jnp.float32),
            pltpu.VMEM((count, tile_users), jnp.bfloat16),
            pltpu.VMEM((count, width), jnp.float32),
        ],
        compiler_params=pltpu.CompilerParams(vmem_limit_bytes=48 * MIB),
        name="tower_and_softmax",
    )(
        me, elig, *pieces, w_hidden, b_hidden.reshape(1, hid), w_out, b_out.reshape(1, width),
        items, positives.reshape(1, users),
    )


def reduce_kernel(
    chips, shards, part_ref, out_ref, got_a, sum_a, got_b, sum_b, got_c,
    send_a, recv_a, send_b, recv_b, send_c, recv_c,
):
    item = lax.axis_index("item")
    shard = lax.axis_index("tbl")
    core = lax.rem(item, 2)
    chip = item // 2
    other_core = (2 * chip + 1 - core, shard)
    chip_at = lambda k: (2 * lax.rem(chip + k, chips) + core, shard)
    shard_at = lambda k: (item, lax.rem(shard + k, shards))
    partners = (
        [other_core]
        + [chip_at(k) for k in range(1, chips)]
        + [shard_at(k) for k in range(1, shards)]
    )
    barrier = pltpu.get_barrier_semaphore()
    for partner in partners:
        pl.semaphore_signal(barrier, inc=1, device_id=partner, device_id_type=MESH)
    pl.semaphore_wait(barrier, len(partners))

    rows = out_ref.shape[0]
    halves = part_ref.shape[0]
    half = part_ref.shape[4]
    first = []
    for h in range(halves):
        first.append(pltpu.make_async_remote_copy(
            src_ref=part_ref.at[h, :, 1 - core], dst_ref=got_a.at[h],
            send_sem=send_a.at[h], recv_sem=recv_a.at[h],
            device_id=other_core, device_id_type=MESH,
        ))
        first[h].start()
    second = []
    for h in range(halves):
        first[h].wait()
        sum_a[h] = (
            part_ref[h, :, core].astype(jnp.float32) + got_a[h].astype(jnp.float32)
        ).astype(sum_a.dtype)
        second.append([])
        for k in range(1, chips):
            second[h].append(pltpu.make_async_remote_copy(
                src_ref=sum_a.at[h, lax.rem(chip + k, chips)], dst_ref=got_b.at[h, k - 1],
                send_sem=send_b.at[h, k - 1], recv_sem=recv_b.at[h, k - 1],
                device_id=chip_at(k), device_id_type=MESH,
            ))
            second[h][-1].start()
    third = []
    for h in range(halves):
        total = sum_a[h, chip].astype(jnp.float32)
        for k in range(1, chips):
            second[h][k - 1].wait()
            total += got_b[h, k - 1].astype(jnp.float32)
        sum_b[h] = total.astype(sum_b.dtype).reshape(shards, rows, half)
        third.append([])
        for k in range(1, shards):
            third[h].append(pltpu.make_async_remote_copy(
                src_ref=sum_b.at[h, lax.rem(shard + k, shards)], dst_ref=got_c.at[h, k - 1],
                send_sem=send_c.at[h, k - 1], recv_sem=recv_c.at[h, k - 1],
                device_id=shard_at(k), device_id_type=MESH,
            ))
            third[h][-1].start()
    for h in range(halves):
        total = sum_b[h, shard].astype(jnp.float32)
        for k in range(1, shards):
            third[h][k - 1].wait()
            total += got_c[h, k - 1].astype(jnp.float32)
        out_ref[:, h * half : (h + 1) * half] = total


def reduce_call(partial):
    halves, chips, _, rows, half = partial.shape
    shards = lax.axis_size("tbl")
    piece = rows // shards
    dma = pltpu.SemaphoreType.DMA
    return pl.pallas_call(
        functools.partial(reduce_kernel, chips, shards),
        out_shape=jax.ShapeDtypeStruct((piece, halves * half), jnp.float32),
        in_specs=[pl.BlockSpec(memory_space=pltpu.VMEM)],
        out_specs=pl.BlockSpec(memory_space=pltpu.VMEM),
        scratch_shapes=[
            pltpu.VMEM((halves, chips, rows, half), jnp.bfloat16),
            pltpu.VMEM((halves, chips, rows, half), jnp.bfloat16),
            pltpu.VMEM((halves, chips - 1, rows, half), jnp.bfloat16),
            pltpu.VMEM((halves, shards, piece, half), jnp.bfloat16),
            pltpu.VMEM((halves, shards - 1, piece, half), jnp.bfloat16),
            dma((halves,)), dma((halves,)),
            dma((halves, chips - 1)), dma((halves, chips - 1)),
            dma((halves, shards - 1)), dma((halves, shards - 1)),
        ],
        compiler_params=pltpu.CompilerParams(
            collective_id=0, has_side_effects=True, vmem_limit_bytes=24 * MIB
        ),
        name="reduce_item_grad",
    )(partial)


def local(
    tables, feat_ids, bag_lens, w_hidden, b_hidden, w_out, b_out, item_vecs, elig_mask, positives
):
    shards = lax.axis_size("tbl")
    me = lax.axis_index("tbl")
    group_users, features, bag = feat_ids.shape
    users = group_users // shards
    rows, width = tables.shape[1:]

    zero_row = features * rows
    table = jnp.pad(tables.reshape(zero_row, width).astype(jnp.float32), ((0, 8), (0, 0)))
    table = lax.optimization_barrier(table).reshape(zero_row + 8, 1, width)
    ids = jnp.transpose(feat_ids, (1, 2, 0))
    lens = jnp.transpose(bag_lens, (1, 0))
    in_bag = jnp.arange(bag, dtype=jnp.int32)[None, :, None] < lens[:, None, :]
    base = (jnp.arange(features, dtype=jnp.int32) * rows)[:, None, None]
    ids = jnp.where(in_bag, ids + base, zero_row)
    ids = jnp.transpose(ids.reshape(features * bag, shards, users), (1, 0, 2))
    ids = ids.reshape(shards, features * bag * users)

    cycle = lax.axis_size("item")
    items = item_vecs
    reach = 1
    order = sorted(range(1, shards), key=lambda d: (abs(2 * d - shards), d)) + [0]
    pieces = []
    for distance in order:
        target = lax.rem(me + distance, shards)
        chunk = lax.dynamic_index_in_dim(ids, target, 0, keepdims=False)
        arrived = None
        if reach < cycle:
            pairs = [(source, source ^ reach) for source in range(cycle)]
            arrived = lax.ppermute(items, "item", pairs)
            reach *= 2
        pooled = pool_chunk(chunk, table, users, features, bag)
        if arrived is not None:
            arrived, pooled = lax.optimization_barrier((arrived, pooled))
            items = jnp.concatenate([items, arrived])
        if distance:
            pairs = [(source, (source + distance) % shards) for source in range(shards)]
            pooled = lax.ppermute(pooled, "tbl", pairs)
        pieces.append(pooled)
    assert reach == cycle

    loss, user_grad, partial = main_call(
        tuple(order), item_vecs.shape[0],
        jnp.stack([me, lax.axis_index("item")]).astype(jnp.int32), pieces, w_hidden, b_hidden, w_out, b_out,
        items, elig_mask, positives,
    )
    partial = partial.reshape(2, cycle // 2, 2, item_vecs.shape[0], item_vecs.shape[1] // 2)
    item_grad = reduce_call(partial)
    return (loss.reshape(users), user_grad, item_grad)


def solution(mesh):
    in_specs = (
        P("tbl", None, None),
        P("item", "tbl", None),
        P("item", "tbl"),
        P(),
        P(),
        P(),
        P(),
        P("item", None),
        P(("item", "tbl"), None),
        P(("item", "tbl")),
    )
    out_specs = (P(("item", "tbl")), P(("item", "tbl"), None), P(("item", "tbl"), None))
    return jax.shard_map(local, mesh=mesh, in_specs=in_specs, out_specs=out_specs, check_vma=False)
```

```python
import functools

import jax
import jax.numpy as jnp
from jax import lax
from jax.experimental import pallas as pl
from jax.experimental.pallas import tpu as pltpu
from jax.sharding import PartitionSpec as P

masked_value = -1e30
UNROLL = 32
MIB = 1 << 20
MESH = pl.DeviceIdType.MESH


def pool_kernel(features, bag, ids_ref, table_ref, out_ref, sums_ref):
    users = out_ref.shape[0]
    width = table_ref.shape[1]
    row_ref = table_ref.reshape(table_ref.shape[0], 1, width)

    def group(step, carry):
        first = pl.multiple_of(step * UNROLL, UNROLL)
        for user in range(UNROLL):
            for feature in range(features):
                rows = []
                for entry in range(bag // 2):
                    pair = ids_ref[first + ((feature * (bag // 2) + entry) * users + user)]
                    rows += [row_ref[pair & 0xFFFF], row_ref[pair >> 16]]
                while len(rows) > 1:
                    rows = [
                        rows[k] + rows[k + 1] if k + 1 < len(rows) else rows[k]
                        for k in range(0, len(rows), 2)
                    ]
                sums_ref[step, user : user + 1, feature * width : (feature + 1) * width] = rows[0]
        return carry

    lax.fori_loop(0, users // UNROLL, group, 0)
    out_ref[...] = sums_ref[...].reshape(out_ref.shape).astype(out_ref.dtype)


def pool_chunk(ids, table, users, features, bag):
    width = table.shape[1]
    return pl.pallas_call(
        functools.partial(pool_kernel, features, bag),
        out_shape=jax.ShapeDtypeStruct((users, features * width), jnp.bfloat16),
        in_specs=[
            pl.BlockSpec(memory_space=pltpu.SMEM),
            pl.BlockSpec(memory_space=pltpu.VMEM),
        ],
        out_specs=pl.BlockSpec(memory_space=pltpu.VMEM),
        scratch_shapes=[pltpu.VMEM((users // UNROLL, UNROLL, features * width), jnp.float32)],
        compiler_params=pltpu.CompilerParams(vmem_limit_bytes=12 * MIB),
        cost_estimate=pl.CostEstimate(
            flops=users * features * bag * width * 100, bytes_accessed=16 * MIB, transcendentals=0
        ),
        name="pool_chunk",
    )(ids, table)


def main_kernel(order, owned, chips, me_ref, elig_ref, *refs):
    count = len(order)
    piece_refs, refs = refs[:count], refs[count:]
    held_refs, refs = refs[:chips], refs[chips:]
    (w1_ref, b1_ref, w2_ref, b2_ref, pos_ref, loss_ref, ugrad_ref, igrad_ref,
     items_ref, scores_ref, signal_ref, acc_ref) = refs
    tile = pl.program_id(0)
    tile_users = ugrad_ref.shape[0]
    items = items_ref.shape[0]
    blocks = elig_ref.shape[1]
    iblk = items // blocks
    user_block = tile * elig_ref.shape[0] // pl.num_programs(0)
    depth = piece_refs[0].shape[1]
    me = me_ref[0]

    @pl.when(tile == 0)
    def _():
        for offset in range(items // owned):
            place = pl.multiple_of((me_ref[1] ^ offset) * owned, owned)
            lower = offset % 2 * owned
            items_ref[pl.ds(place, owned), :] = held_refs[offset // 2][lower : lower + owned, :]

    hidden = None
    for position, distance in enumerate(order):
        source = lax.rem(me - distance + count, count)
        weight = w1_ref[pl.ds(pl.multiple_of(source * depth, depth), depth), :]
        part = jnp.dot(piece_refs[position][...], weight, preferred_element_type=jnp.float32)
        hidden = part if hidden is None else hidden + part
    hidden = jnp.maximum(hidden + b1_ref[...], 0.0).astype(jnp.bfloat16)
    queries = (
        jnp.dot(hidden, w2_ref[...], preferred_element_type=jnp.float32) + b2_ref[...]
    ).astype(jnp.bfloat16)

    wanted = pos_ref[...]
    row = lax.broadcasted_iota(jnp.int32, (iblk, tile_users), 0)
    peak = jnp.full((8, tile_users), masked_value, jnp.float32)
    chosen = jnp.zeros((8, tile_users), jnp.float32)
    for block in range(blocks):
        span = slice(block * iblk, (block + 1) * iblk)
        scores = lax.dot_general(
            items_ref[span, :], queries, (((1,), (1,)), ((), ())),
            preferred_element_type=jnp.float32,
        )
        scores = jnp.where(elig_ref[user_block, block] > 0, scores, masked_value)
        target = row == wanted - block * iblk
        chosen += jnp.sum(
            jnp.where(target, scores, 0.0).reshape(iblk // 8, 8, tile_users), axis=0
        )
        peak = jnp.maximum(peak, jnp.max(scores.reshape(iblk // 8, 8, tile_users), axis=0))
        scores_ref[span, :] = scores
    peak = jnp.max(peak, axis=0, keepdims=True)
    chosen = jnp.sum(chosen, axis=0, keepdims=True)
    total = jnp.zeros((8, tile_users), jnp.float32)
    for block in range(blocks):
        span = slice(block * iblk, (block + 1) * iblk)
        weights = jnp.exp(scores_ref[span, :] - peak)
        total += jnp.sum(weights.reshape(iblk // 8, 8, tile_users), axis=0)
        scores_ref[span, :] = weights
    total = jnp.sum(total, axis=0, keepdims=True)
    loss_ref[...] = peak + jnp.log(total) - chosen
    inverse = 1.0 / total
    for block in range(blocks):
        span = slice(block * iblk, (block + 1) * iblk)
        target = row == wanted - block * iblk
        signal_ref[span, :] = (
            scores_ref[span, :] * inverse - target.astype(jnp.float32)
        ).astype(jnp.bfloat16)
    ugrad_ref[...] = lax.dot_general(
        signal_ref[...], items_ref[...], (((0,), (0,)), ((), ())),
        preferred_element_type=jnp.float32,
    )
    part = jnp.dot(signal_ref[...], queries, preferred_element_type=jnp.float32)

    @pl.when(tile == 0)
    def _():
        acc_ref[...] = part

    @pl.when(tile > 0)
    def _():
        acc_ref[...] += part

    @pl.when(tile == pl.num_programs(0) - 1)
    def _():
        half = igrad_ref.shape[2]
        for h in range(igrad_ref.shape[0]):
            igrad_ref[h] = acc_ref[:, h * half : (h + 1) * half].astype(igrad_ref.dtype)


def main_call(order, owned, me, pieces, w_hidden, b_hidden, w_out, b_out, held, elig, positives):
    users, depth = pieces[0].shape
    tile_users = 256
    tiles = users // tile_users
    width = w_out.shape[1]
    count = sum(block.shape[0] for block in held)
    hid = w_hidden.shape[1]
    whole = lambda shape: pl.BlockSpec(shape, lambda i: (0, 0))
    smem = pl.BlockSpec(memory_space=pltpu.SMEM)
    return pl.pallas_call(
        functools.partial(main_kernel, order, owned, len(held)),
        grid=(tiles,),
        out_shape=(
            jax.ShapeDtypeStruct((1, users), jnp.float32),
            jax.ShapeDtypeStruct((users, width), jnp.float32),
            jax.ShapeDtypeStruct((2, count, width // 2), jnp.bfloat16),
        ),
        in_specs=[smem, smem]
        + [pl.BlockSpec((tile_users, depth), lambda i: (i, 0))] * len(order)
        + [whole(block.shape) for block in held]
        + [
            whole(w_hidden.shape),
            whole((1, hid)),
            whole(w_out.shape),
            whole((1, width)),
            pl.BlockSpec((1, tile_users), lambda i: (0, i)),
        ],
        out_specs=(
            pl.BlockSpec((1, tile_users), lambda i: (0, i)),
            pl.BlockSpec((tile_users, width), lambda i: (i, 0)),
            pl.BlockSpec((2, count, width // 2), lambda i: (0, 0, 0)),
        ),
        scratch_shapes=[
            pltpu.VMEM((count, width), jnp.bfloat16),
            pltpu.VMEM((count, tile_users), jnp.float32),
            pltpu.VMEM((count, tile_users), jnp.bfloat16),
            pltpu.VMEM((count, width), jnp.float32),
        ],
        compiler_params=pltpu.CompilerParams(vmem_limit_bytes=48 * MIB),
        name="tower_and_softmax",
    )(
        me, elig, *pieces, *held, w_hidden, b_hidden.reshape(1, hid), w_out, b_out.reshape(1, width),
        positives.reshape(1, users),
    )


def reduce_kernel(
    chips, shards, part_ref, out_ref, got_a, sum_a, got_b, sum_b, got_c,
    send_a, recv_a, send_b, recv_b, send_c, recv_c,
):
    item = lax.axis_index("item")
    shard = lax.axis_index("tbl")
    core = lax.rem(item, 2)
    chip = item // 2
    other_core = (2 * chip + 1 - core, shard)
    chip_at = lambda k: (2 * lax.rem(chip + k, chips) + core, shard)
    shard_at = lambda k: (item, lax.rem(shard + k, shards))
    partners = (
        [other_core]
        + [chip_at(k) for k in range(1, chips)]
        + [shard_at(k) for k in range(1, shards)]
    )
    barrier = pltpu.get_barrier_semaphore()
    for partner in partners:
        pl.semaphore_signal(barrier, inc=1, device_id=partner, device_id_type=MESH)
    pl.semaphore_wait(barrier, len(partners))

    rows = out_ref.shape[0]
    halves = part_ref.shape[0]
    half = part_ref.shape[4]
    first = []
    for h in range(halves):
        first.append(pltpu.make_async_remote_copy(
            src_ref=part_ref.at[h, :, 1 - core], dst_ref=got_a.at[h],
            send_sem=send_a.at[h], recv_sem=recv_a.at[h],
            device_id=other_core, device_id_type=MESH,
        ))
        first[h].start()
    second = []
    for h in range(halves):
        first[h].wait()
        sum_a[h] = (
            part_ref[h, :, core].astype(jnp.float32) + got_a[h].astype(jnp.float32)
        ).astype(sum_a.dtype)
        second.append([])
        for k in range(1, chips):
            second[h].append(pltpu.make_async_remote_copy(
                src_ref=sum_a.at[h, lax.rem(chip + k, chips)], dst_ref=got_b.at[h, k - 1],
                send_sem=send_b.at[h, k - 1], recv_sem=recv_b.at[h, k - 1],
                device_id=chip_at(k), device_id_type=MESH,
            ))
            second[h][-1].start()
    third = []
    for h in range(halves):
        total = sum_a[h, chip].astype(jnp.float32)
        for k in range(1, chips):
            second[h][k - 1].wait()
            total += got_b[h, k - 1].astype(jnp.float32)
        sum_b[h] = total.astype(sum_b.dtype).reshape(shards, rows, half)
        third.append([])
        for k in range(1, shards):
            third[h].append(pltpu.make_async_remote_copy(
                src_ref=sum_b.at[h, lax.rem(shard + k, shards)], dst_ref=got_c.at[h, k - 1],
                send_sem=send_c.at[h, k - 1], recv_sem=recv_c.at[h, k - 1],
                device_id=shard_at(k), device_id_type=MESH,
            ))
            third[h][-1].start()
    for h in range(halves):
        total = sum_b[h, shard].astype(jnp.float32)
        for k in range(1, shards):
            third[h][k - 1].wait()
            total += got_c[h, k - 1].astype(jnp.float32)
        out_ref[:, h * half : (h + 1) * half] = total


def reduce_call(partial):
    halves, chips, _, rows, half = partial.shape
    shards = lax.axis_size("tbl")
    piece = rows // shards
    dma = pltpu.SemaphoreType.DMA
    return pl.pallas_call(
        functools.partial(reduce_kernel, chips, shards),
        out_shape=jax.ShapeDtypeStruct((piece, halves * half), jnp.float32),
        in_specs=[pl.BlockSpec(memory_space=pltpu.VMEM)],
        out_specs=pl.BlockSpec(memory_space=pltpu.VMEM),
        scratch_shapes=[
            pltpu.VMEM((halves, chips, rows, half), jnp.bfloat16),
            pltpu.VMEM((halves, chips, rows, half), jnp.bfloat16),
            pltpu.VMEM((halves, chips - 1, rows, half), jnp.bfloat16),
            pltpu.VMEM((halves, shards, piece, half), jnp.bfloat16),
            pltpu.VMEM((halves, shards - 1, piece, half), jnp.bfloat16),
            dma((halves,)), dma((halves,)),
            dma((halves, chips - 1)), dma((halves, chips - 1)),
            dma((halves, shards - 1)), dma((halves, shards - 1)),
        ],
        compiler_params=pltpu.CompilerParams(
            collective_id=0, has_side_effects=True, vmem_limit_bytes=24 * MIB
        ),
        name="reduce_item_grad",
    )(partial)


def local(
    tables, feat_ids, bag_lens, w_hidden, b_hidden, w_out, b_out, item_vecs, elig_mask, positives
):
    shards = lax.axis_size("tbl")
    me = lax.axis_index("tbl")
    group_users, features, bag = feat_ids.shape
    users = group_users // shards
    rows, width = tables.shape[1:]

    zero_row = features * rows
    table = jnp.pad(tables.reshape(zero_row, width).astype(jnp.float32), ((0, 8), (0, 0)))
    ids = jnp.transpose(feat_ids, (1, 2, 0))
    lens = jnp.transpose(bag_lens, (1, 0))
    in_bag = jnp.arange(bag, dtype=jnp.int32)[None, :, None] < lens[:, None, :]
    base = (jnp.arange(features, dtype=jnp.int32) * rows)[:, None, None]
    ids = jnp.where(in_bag, ids + base, zero_row)
    assert zero_row < 1 << 15 and bag % 2 == 0
    ids = ids[:, : bag // 2, :] + (ids[:, bag // 2 :, :] << 16)
    words = features * bag // 2
    ids = jnp.transpose(ids.reshape(words, shards, users), (1, 0, 2)).reshape(shards, words * users)

    cycle = lax.axis_size("item")
    swap = lambda value, reach: lax.ppermute(
        value, "item", [(source, source ^ reach) for source in range(cycle)]
    )
    own = jnp.concatenate([item_vecs, swap(item_vecs, 1)])
    held = [own] + [swap(own, 2 * k) for k in range(1, cycle // 2)]
    order = sorted(range(1, shards), key=lambda d: (abs(2 * d - shards), d)) + [0]
    pieces = []
    for distance in order:
        target = lax.rem(me + distance, shards)
        chunk = lax.dynamic_index_in_dim(ids, target, 0, keepdims=False)
        pooled = pool_chunk(chunk, table, users, features, bag)
        if distance:
            pairs = [(source, (source + distance) % shards) for source in range(shards)]
            pooled = lax.ppermute(pooled, "tbl", pairs)
        pieces.append(pooled)

    loss, user_grad, partial = main_call(
        tuple(order), item_vecs.shape[0],
        jnp.stack([me, lax.axis_index("item")]).astype(jnp.int32), pieces, w_hidden, b_hidden, w_out, b_out,
        held, elig_mask, positives,
    )
    partial = partial.reshape(2, cycle // 2, 2, item_vecs.shape[0], item_vecs.shape[1] // 2)
    item_grad = reduce_call(partial)
    return (loss.reshape(users), user_grad, item_grad)


def solution(mesh):
    in_specs = (
        P("tbl", None, None),
        P("item", "tbl", None),
        P("item", "tbl"),
        P(),
        P(),
        P(),
        P(),
        P("item", None),
        P(("item", "tbl"), None),
        P(("item", "tbl")),
    )
    out_specs = (P(("item", "tbl")), P(("item", "tbl"), None), P(("item", "tbl"), None))
    return jax.shard_map(local, mesh=mesh, in_specs=in_specs, out_specs=out_specs, check_vma=False)
```

```python
import functools

import jax
import jax.numpy as jnp
from jax import lax
from jax.experimental import pallas as pl
from jax.experimental.pallas import tpu as pltpu
from jax.sharding import PartitionSpec as P

masked_value = -1e30
UNROLL = 32
MIB = 1 << 20
MESH = pl.DeviceIdType.MESH


def pool_kernel(features, bag, ids_ref, table_ref, out_ref, sums_ref):
    users = out_ref.shape[0]
    width = table_ref.shape[1]
    row_ref = table_ref.reshape(table_ref.shape[0], 1, width)

    def group(step, carry):
        first = pl.multiple_of(step * UNROLL, UNROLL)
        for user in range(UNROLL):
            for feature in range(features):
                rows = []
                for entry in range(bag // 2):
                    pair = ids_ref[first + ((feature * (bag // 2) + entry) * users + user)]
                    rows += [row_ref[pair & 0xFFFF], row_ref[pair >> 16]]
                while len(rows) > 1:
                    rows = [
                        rows[k] + rows[k + 1] if k + 1 < len(rows) else rows[k]
                        for k in range(0, len(rows), 2)
                    ]
                sums_ref[step, user : user + 1, feature * width : (feature + 1) * width] = rows[0]
        return carry

    lax.fori_loop(0, users // UNROLL, group, 0)
    out_ref[...] = sums_ref[...].reshape(out_ref.shape).astype(out_ref.dtype)


def pool_chunk(ids, table, users, features, bag):
    width = table.shape[1]
    return pl.pallas_call(
        functools.partial(pool_kernel, features, bag),
        out_shape=jax.ShapeDtypeStruct((users, features * width), jnp.bfloat16),
        in_specs=[
            pl.BlockSpec(memory_space=pltpu.SMEM),
            pl.BlockSpec(memory_space=pltpu.VMEM),
        ],
        out_specs=pl.BlockSpec(memory_space=pltpu.VMEM),
        scratch_shapes=[pltpu.VMEM((users // UNROLL, UNROLL, features * width), jnp.float32)],
        compiler_params=pltpu.CompilerParams(vmem_limit_bytes=12 * MIB),
        cost_estimate=pl.CostEstimate(
            flops=users * features * bag * width * 100, bytes_accessed=16 * MIB, transcendentals=0
        ),
        name="pool_chunk",
    )(ids, table)


def main_kernel(order, owned, chips, me_ref, elig_ref, *refs):
    count = len(order)
    piece_refs, refs = refs[:count], refs[count:]
    held_refs, refs = refs[:chips], refs[chips:]
    (w1_ref, b1_ref, w2_ref, b2_ref, pos_ref, loss_ref, ugrad_ref, igrad_ref,
     items_ref, scores_ref, signal_ref, acc_ref) = refs
    tile = pl.program_id(0)
    tile_users = ugrad_ref.shape[0]
    items = items_ref.shape[0]
    blocks = elig_ref.shape[1]
    iblk = items // blocks
    user_block = tile * elig_ref.shape[0] // pl.num_programs(0)
    depth = piece_refs[0].shape[1]
    me = me_ref[0]

    @pl.when(tile == 0)
    def _():
        for offset in range(items // owned):
            place = pl.multiple_of((me_ref[1] ^ offset) * owned, owned)
            lower = offset % 2 * owned
            items_ref[pl.ds(place, owned), :] = held_refs[offset // 2][lower : lower + owned, :]

    hidden = None
    for position, distance in enumerate(order):
        source = lax.rem(me - distance + count, count)
        weight = w1_ref[pl.ds(pl.multiple_of(source * depth, depth), depth), :]
        part = jnp.dot(piece_refs[position][...], weight, preferred_element_type=jnp.float32)
        hidden = part if hidden is None else hidden + part
    hidden = jnp.maximum(hidden + b1_ref[...], 0.0).astype(jnp.bfloat16)
    queries = (
        jnp.dot(hidden, w2_ref[...], preferred_element_type=jnp.float32) + b2_ref[...]
    ).astype(jnp.bfloat16)

    wanted = pos_ref[...]
    row = lax.broadcasted_iota(jnp.int32, (iblk, tile_users), 0)
    peak = jnp.full((8, tile_users), masked_value, jnp.float32)
    chosen = jnp.zeros((8, tile_users), jnp.float32)
    for block in range(blocks):
        span = slice(block * iblk, (block + 1) * iblk)
        scores = lax.dot_general(
            items_ref[span, :], queries, (((1,), (1,)), ((), ())),
            preferred_element_type=jnp.float32,
        )
        scores = jnp.where(elig_ref[user_block, block] > 0, scores, masked_value)
        target = row == wanted - block * iblk
        chosen += jnp.sum(
            jnp.where(target, scores, 0.0).reshape(iblk // 8, 8, tile_users), axis=0
        )
        peak = jnp.maximum(peak, jnp.max(scores.reshape(iblk // 8, 8, tile_users), axis=0))
        scores_ref[span, :] = scores
    peak = jnp.max(peak, axis=0, keepdims=True)
    chosen = jnp.sum(chosen, axis=0, keepdims=True)
    total = jnp.zeros((8, tile_users), jnp.float32)
    for block in range(blocks):
        span = slice(block * iblk, (block + 1) * iblk)
        weights = jnp.exp(scores_ref[span, :] - peak)
        total += jnp.sum(weights.reshape(iblk // 8, 8, tile_users), axis=0)
        scores_ref[span, :] = weights
    total = jnp.sum(total, axis=0, keepdims=True)
    loss_ref[...] = peak + jnp.log(total) - chosen
    inverse = 1.0 / total
    for block in range(blocks):
        span = slice(block * iblk, (block + 1) * iblk)
        target = row == wanted - block * iblk
        signal_ref[span, :] = (
            scores_ref[span, :] * inverse - target.astype(jnp.float32)
        ).astype(jnp.bfloat16)
    ugrad_ref[...] = lax.dot_general(
        signal_ref[...], items_ref[...], (((0,), (0,)), ((), ())),
        preferred_element_type=jnp.float32,
    )
    part = jnp.dot(signal_ref[...], queries, preferred_element_type=jnp.float32)

    @pl.when(tile == 0)
    def _():
        acc_ref[...] = part

    @pl.when(tile > 0)
    def _():
        acc_ref[...] += part

    @pl.when(tile == pl.num_programs(0) - 1)
    def _():
        half = igrad_ref.shape[2]
        for h in range(igrad_ref.shape[0]):
            igrad_ref[h] = acc_ref[:, h * half : (h + 1) * half].astype(igrad_ref.dtype)


def main_call(order, owned, me, pieces, w_hidden, b_hidden, w_out, b_out, held, elig, positives):
    users, depth = pieces[0].shape
    tile_users = users // elig.shape[0]
    tiles = users // tile_users
    width = w_out.shape[1]
    count = sum(block.shape[0] for block in held)
    hid = w_hidden.shape[1]
    whole = lambda shape: pl.BlockSpec(shape, lambda i: (0, 0))
    smem = pl.BlockSpec(memory_space=pltpu.SMEM)
    return pl.pallas_call(
        functools.partial(main_kernel, order, owned, len(held)),
        grid=(tiles,),
        out_shape=(
            jax.ShapeDtypeStruct((1, users), jnp.float32),
            jax.ShapeDtypeStruct((users, width), jnp.float32),
            jax.ShapeDtypeStruct((2, count, width // 2), jnp.bfloat16),
        ),
        in_specs=[smem, smem]
        + [pl.BlockSpec((tile_users, depth), lambda i: (i, 0))] * len(order)
        + [whole(block.shape) for block in held]
        + [
            whole(w_hidden.shape),
            whole((1, hid)),
            whole(w_out.shape),
            whole((1, width)),
            pl.BlockSpec((1, tile_users), lambda i: (0, i)),
        ],
        out_specs=(
            pl.BlockSpec((1, tile_users), lambda i: (0, i)),
            pl.BlockSpec((tile_users, width), lambda i: (i, 0)),
            pl.BlockSpec((2, count, width // 2), lambda i: (0, 0, 0)),
        ),
        scratch_shapes=[
            pltpu.VMEM((count, width), jnp.bfloat16),
            pltpu.VMEM((count, tile_users), jnp.float32),
            pltpu.VMEM((count, tile_users), jnp.bfloat16),
            pltpu.VMEM((count, width), jnp.float32),
        ],
        compiler_params=pltpu.CompilerParams(vmem_limit_bytes=48 * MIB),
        name="tower_and_softmax",
    )(
        me, elig, *pieces, *held, w_hidden, b_hidden.reshape(1, hid), w_out, b_out.reshape(1, width),
        positives.reshape(1, users),
    )


def reduce_kernel(
    chips, shards, part_ref, out_ref, got_a, sum_a, got_b, sum_b, got_c,
    send_a, recv_a, send_b, recv_b, send_c, recv_c,
):
    item = lax.axis_index("item")
    shard = lax.axis_index("tbl")
    core = lax.rem(item, 2)
    chip = item // 2
    other_core = (2 * chip + 1 - core, shard)
    chip_at = lambda k: (2 * lax.rem(chip + k, chips) + core, shard)
    shard_at = lambda k: (item, lax.rem(shard + k, shards))
    partners = (
        [other_core]
        + [chip_at(k) for k in range(1, chips)]
        + [shard_at(k) for k in range(1, shards)]
    )
    barrier = pltpu.get_barrier_semaphore()
    for partner in partners:
        pl.semaphore_signal(barrier, inc=1, device_id=partner, device_id_type=MESH)
    pl.semaphore_wait(barrier, len(partners))

    rows = out_ref.shape[0]
    halves = part_ref.shape[0]
    half = part_ref.shape[4]
    first = []
    for h in range(halves):
        first.append(pltpu.make_async_remote_copy(
            src_ref=part_ref.at[h, :, 1 - core], dst_ref=got_a.at[h],
            send_sem=send_a.at[h], recv_sem=recv_a.at[h],
            device_id=other_core, device_id_type=MESH,
        ))
        first[h].start()
    second = []
    for h in range(halves):
        first[h].wait()
        sum_a[h] = (
            part_ref[h, :, core].astype(jnp.float32) + got_a[h].astype(jnp.float32)
        ).astype(sum_a.dtype)
        second.append([])
        for k in range(1, chips):
            second[h].append(pltpu.make_async_remote_copy(
                src_ref=sum_a.at[h, lax.rem(chip + k, chips)], dst_ref=got_b.at[h, k - 1],
                send_sem=send_b.at[h, k - 1], recv_sem=recv_b.at[h, k - 1],
                device_id=chip_at(k), device_id_type=MESH,
            ))
            second[h][-1].start()
    third = []
    for h in range(halves):
        total = sum_a[h, chip].astype(jnp.float32)
        for k in range(1, chips):
            second[h][k - 1].wait()
            total += got_b[h, k - 1].astype(jnp.float32)
        sum_b[h] = total.astype(sum_b.dtype).reshape(shards, rows, half)
        third.append([])
        for k in range(1, shards):
            third[h].append(pltpu.make_async_remote_copy(
                src_ref=sum_b.at[h, lax.rem(shard + k, shards)], dst_ref=got_c.at[h, k - 1],
                send_sem=send_c.at[h, k - 1], recv_sem=recv_c.at[h, k - 1],
                device_id=shard_at(k), device_id_type=MESH,
            ))
            third[h][-1].start()
    for h in range(halves):
        total = sum_b[h, shard].astype(jnp.float32)
        for k in range(1, shards):
            third[h][k - 1].wait()
            total += got_c[h, k - 1].astype(jnp.float32)
        out_ref[:, h * half : (h + 1) * half] = total


def reduce_call(partial):
    halves, chips, _, rows, half = partial.shape
    shards = lax.axis_size("tbl")
    piece = rows // shards
    dma = pltpu.SemaphoreType.DMA
    return pl.pallas_call(
        functools.partial(reduce_kernel, chips, shards),
        out_shape=jax.ShapeDtypeStruct((piece, halves * half), jnp.float32),
        in_specs=[pl.BlockSpec(memory_space=pltpu.VMEM)],
        out_specs=pl.BlockSpec(memory_space=pltpu.VMEM),
        scratch_shapes=[
            pltpu.VMEM((halves, chips, rows, half), jnp.bfloat16),
            pltpu.VMEM((halves, chips, rows, half), jnp.bfloat16),
            pltpu.VMEM((halves, chips - 1, rows, half), jnp.bfloat16),
            pltpu.VMEM((halves, shards, piece, half), jnp.bfloat16),
            pltpu.VMEM((halves, shards - 1, piece, half), jnp.bfloat16),
            dma((halves,)), dma((halves,)),
            dma((halves, chips - 1)), dma((halves, chips - 1)),
            dma((halves, shards - 1)), dma((halves, shards - 1)),
        ],
        compiler_params=pltpu.CompilerParams(
            collective_id=0, has_side_effects=True, vmem_limit_bytes=24 * MIB
        ),
        name="reduce_item_grad",
    )(partial)


def local(
    tables, feat_ids, bag_lens, w_hidden, b_hidden, w_out, b_out, item_vecs, elig_mask, positives
):
    shards = lax.axis_size("tbl")
    me = lax.axis_index("tbl")
    group_users, features, bag = feat_ids.shape
    users = group_users // shards
    rows, width = tables.shape[1:]

    zero_row = features * rows
    table = jnp.pad(tables.reshape(zero_row, width).astype(jnp.float32), ((0, 8), (0, 0)))
    ids = jnp.transpose(feat_ids, (1, 2, 0))
    lens = jnp.transpose(bag_lens, (1, 0))
    in_bag = jnp.arange(bag, dtype=jnp.int32)[None, :, None] < lens[:, None, :]
    base = (jnp.arange(features, dtype=jnp.int32) * rows)[:, None, None]
    ids = jnp.where(in_bag, ids + base, zero_row)
    assert zero_row < 1 << 15 and bag % 2 == 0
    ids = ids[:, : bag // 2, :] + (ids[:, bag // 2 :, :] << 16)
    words = features * bag // 2
    ids = jnp.transpose(ids.reshape(words, shards, users), (1, 0, 2)).reshape(shards, words * users)

    cycle = lax.axis_size("item")
    swap = lambda value, reach: lax.ppermute(
        value, "item", [(source, source ^ reach) for source in range(cycle)]
    )
    own = jnp.concatenate([item_vecs, swap(item_vecs, 1)])
    held = [own] + [swap(own, 2 * k) for k in range(1, cycle // 2)]
    order = sorted(range(1, shards), key=lambda d: (abs(2 * d - shards), d)) + [0]
    pieces = []
    for distance in order:
        target = lax.rem(me + distance, shards)
        chunk = lax.dynamic_index_in_dim(ids, target, 0, keepdims=False)
        pooled = pool_chunk(chunk, table, users, features, bag)
        if distance:
            pairs = [(source, (source + distance) % shards) for source in range(shards)]
            pooled = lax.ppermute(pooled, "tbl", pairs)
        pieces.append(pooled)

    loss, user_grad, partial = main_call(
        tuple(order), item_vecs.shape[0],
        jnp.stack([me, lax.axis_index("item")]).astype(jnp.int32), pieces, w_hidden, b_hidden, w_out, b_out,
        held, elig_mask, positives,
    )
    partial = partial.reshape(2, cycle // 2, 2, item_vecs.shape[0], item_vecs.shape[1] // 2)
    item_grad = reduce_call(partial)
    return (loss.reshape(users), user_grad, item_grad)


def solution(mesh):
    in_specs = (
        P("tbl", None, None),
        P("item", "tbl", None),
        P("item", "tbl"),
        P(),
        P(),
        P(),
        P(),
        P("item", None),
        P(("item", "tbl"), None),
        P(("item", "tbl")),
    )
    out_specs = (P(("item", "tbl")), P(("item", "tbl"), None), P(("item", "tbl"), None))
    return jax.shard_map(local, mesh=mesh, in_specs=in_specs, out_specs=out_specs, check_vma=False)
```
